128 devices in a mesh: energy: 8 (over x, core), length: 16 (over y, z).
Axes of the slice: x: 4, y: 4, z: 4, core: 2. Of those that a mesh axis runs over, the one named last changes fastest.
Arguments:
- green_left: float32 [8, 64, 2, 512, 512], P('energy', 'length')
- coupling: float32 [64, 512, 512], P('length')
- pattern: int32 [64, 8, 8], P('length'), may hold values from 0 to 1, as said below
- injection: float32 [8, 2, 512, 64], P('energy'), may hold values from -6 to 6
- weights: float32 [8], P('energy'), may hold values from 0.5 to 2
Outputs:
- charge: float32 [64, 512], P('length', 'energy')
The draws below stay inside these ranges and needn't reach their ends.
Inputs may be any that keep to these rules, and one draw needn't show every extreme that they name: `pattern`: in every block the tiles on the diagonal are 1.
All inputs are finite; a program needn't handle non-finite values.
Results may differ from the reference program's by a relative error of at most 0.00016.
Values sent between devices are 32-bit elements; how exact they have to be, the bound alone decides.
A program may use at most 128 MiB of HBM per device.

```python
import math
import jax
import jax.numpy as jnp
from jax import lax

ORB = 512
TILES = 8
TILE = 64
MODES = 64
BLOCKS = 64
ENERGIES = 8


def draw_green_left(key, part):
    key = jax.random.fold_in(key, 11)
    phase_key, noise_key = jax.random.split(key, 2)
    phases = jax.random.uniform(phase_key, (ENERGIES, BLOCKS, 1, ORB, 1), jnp.float32, -math.pi, math.pi)
    shape_full = (ENERGIES, BLOCKS, 2, ORB, ORB)
    noise_part = jax.random.normal(noise_key, shape_full, jnp.float32)
    row_index = lax.broadcasted_iota(jnp.int32, (ORB, ORB), 0)
    col_index = lax.broadcasted_iota(jnp.int32, (ORB, ORB), 1)
    diagonal = (row_index == col_index).astype(jnp.float32)
    phase_parts = jnp.concatenate([jnp.cos(phases), jnp.sin(phases)], axis=2)
    return 0.969 * (phase_parts * diagonal + 0.18 * noise_part / math.sqrt(ORB))


def draw_coupling(key, part):
    key = jax.random.fold_in(key, 23)
    scale_key, noise_key = jax.random.split(key, 2)
    scales = jnp.exp(jax.random.uniform(scale_key, (BLOCKS, ORB, 1), jnp.float32, math.log(0.7), math.log(1.4)))
    shape_full = (BLOCKS, ORB, ORB)
    noise_part = jax.random.normal(noise_key, shape_full, jnp.float32)
    row_index = lax.broadcasted_iota(jnp.int32, (ORB, ORB), 0)
    col_index = lax.broadcasted_iota(jnp.int32, (ORB, ORB), 1)
    diagonal = (row_index == col_index).astype(jnp.float32)
    return 0.944 * (scales * diagonal + 0.333 * noise_part / math.sqrt(ORB))


def draw_pattern(key, part):
    key = jax.random.fold_in(key, 37)
    random_bits = jax.random.randint(key, (BLOCKS, TILES, TILES), 0, 2)
    row_index = lax.broadcasted_iota(jnp.int32, (TILES, TILES), 0)
    col_index = lax.broadcasted_iota(jnp.int32, (TILES, TILES), 1)
    return jnp.where(row_index == col_index, 1, random_bits).astype(jnp.int32)


def steps_of(stream_key, extent, pieces, low, largest):
    loudness, own = 1.0, jax.random.fold_in(stream_key, 6)
    for position, shards_of in pieces:
        steps = jnp.exp(jax.random.uniform(jax.random.fold_in(own, position), (shards_of,), jnp.float32, low / len(pieces), largest / len(pieces)))
        loudness = loudness * jnp.repeat(steps, extent[position] // shards_of).reshape([-1 if axis == position else 1 for axis in range(len(extent))])
    return loudness


def centred(own_key, shape, spread, limit, shards=(), kind=jnp.bfloat16):
    entries = jax.random.normal(own_key, shape, jnp.float32) * spread
    if len(shards) > 0:
        entries = steps_of(own_key, shape, shards, -0.22, 0.18) * entries
    return jnp.clip(entries, min=-limit, max=limit).astype(kind)


def setup_inputs(seed: int = 0) -> dict:
    keys = jax.random.split(jax.random.key(seed), 6)
    return {
        "green_left": draw_green_left(jax.random.fold_in(keys[5], 71), 0),
        "coupling": draw_coupling(jax.random.fold_in(keys[5], 71), 0),
        "pattern": draw_pattern(jax.random.fold_in(keys[5], 71), 0),
        "injection": centred(keys[3], (ENERGIES, 2, ORB, MODES), 1.0, 6.0, ((0, 8),), jnp.float32),
        "weights": jnp.clip(jnp.exp(math.log(2.0) - 1.3862944 * jax.random.uniform(keys[4], (ENERGIES,), jnp.float32) ** steps_of(keys[4], (ENERGIES,), ((0, 8),), -0.2, 0.2)), 0.5, 2.0),
    }


def reference(green_left, coupling, pattern, injection, weights):
    highest = lax.Precision.HIGHEST
    tile_mask = jnp.repeat(jnp.repeat(pattern, TILE, axis=1), TILE, axis=2).astype(jnp.float32)
    used_coupling = coupling * tile_mask

    def block_step(wavefunction, inputs):
        green_block, coupling_block = inputs
        mixed_real = jnp.dot(coupling_block, wavefunction[0], precision=highest, preferred_element_type=jnp.float32)
        mixed_imag = jnp.dot(coupling_block, wavefunction[1], precision=highest, preferred_element_type=jnp.float32)
        real_part = jnp.dot(green_block[0], mixed_real, precision=highest, preferred_element_type=jnp.float32) - jnp.dot(green_block[1], mixed_imag, precision=highest, preferred_element_type=jnp.float32)
        imag_part = jnp.dot(green_block[0], mixed_imag, precision=highest, preferred_element_type=jnp.float32) + jnp.dot(green_block[1], mixed_real, precision=highest, preferred_element_type=jnp.float32)
        updated = jnp.stack([real_part, imag_part])
        return updated, jnp.sum(updated * updated, axis=(0, 2))

    def energy_step(running, inputs):
        green_energy, injection_energy, weight_energy = inputs
        unused, densities = lax.scan(block_step, injection_energy, (green_energy, used_coupling), reverse=True)
        return running + weight_energy * densities, None

    running, unused = lax.scan(energy_step, jnp.zeros((BLOCKS, ORB), jnp.float32), (green_left, injection, weights))
    return running / (MODES * ENERGIES)
```

```python
import functools

import jax
import jax.numpy as jnp
from jax import lax
from jax.experimental import pallas as pl
from jax.experimental.pallas import tpu as pltpu
from jax.sharding import PartitionSpec as P

MESH = pl.DeviceIdType.MESH
NN = (((1,), (0,)), ((), ()))
NT = (((1,), (1,)), ((), ()))
ROWS = 8


def split(value):
    high = value.astype(jnp.bfloat16)
    return high, (value - high.astype(jnp.float32)).astype(jnp.bfloat16)


def dot(left, right, dims=NN):
    return lax.dot_general(left, right, dims, preferred_element_type=jnp.float32)


def product(left_high, left_low, right_high, right_low, dims=NN):
    return dot(left_high, right_high, dims) + dot(left_high, right_low, dims) + dot(left_low, right_high, dims)


def narrow_product(wave, right_high, right_low, dims=NN):
    rows = wave.shape[0]
    high, low = split(wave)
    both = dot(jnp.concatenate([high, low], axis=0), right_high, dims)
    return both[:rows] + both[rows:] + dot(high, right_low, dims)


def combine(mixed, count, orbitals):
    mixed = mixed.reshape(count, 2, ROWS, 2 * orbitals)
    real_part = mixed[:, 0, :, :orbitals] - mixed[:, 1, :, orbitals:]
    imag_part = mixed[:, 0, :, orbitals:] + mixed[:, 1, :, :orbitals]
    return jnp.stack([real_part, imag_part], axis=1).reshape(count * 2 * ROWS, orbitals)


def kernel(
    sizes,
    green_hbm,
    coupling_hbm,
    pattern_hbm,
    injection_hbm,
    weights_hbm,
    out_ref,
    green,
    coupling,
    pattern,
    injection,
    weights,
    high,
    low,
    wave_in,
    wave_out,
    part_out,
    part_in,
    load_sem,
    small_sem,
    send_sem,
    recv_sem,
    part_send_sem,
    part_recv_sem,
):
    energies, places, blocks, orbitals, tiles, modes = sizes
    chunks = modes // ROWS
    tile = orbitals // tiles
    energy = lax.axis_index("energy")
    place = lax.axis_index("length")
    last = places - 1

    def load(block):
        return (
            pltpu.make_async_copy(coupling_hbm.at[block], coupling.at[block], load_sem.at[0, block]),
            pltpu.make_async_copy(green_hbm.at[0, block], green.at[block], load_sem.at[1, block]),
        )

    smalls = (
        pltpu.make_async_copy(pattern_hbm, pattern, small_sem.at[0]),
        pltpu.make_async_copy(injection_hbm.at[0], injection, small_sem.at[1]),
        pltpu.make_async_copy(weights_hbm, weights, small_sem.at[2]),
    )
    smalls[0].start()
    smalls[1].start()
    for block in reversed(range(blocks)):
        for copy in load(block):
            copy.start()
    smalls[2].start()

    barrier = pltpu.get_barrier_semaphore()
    ahead = lax.rem(place + last, places)
    behind = lax.rem(place + 1, places)
    for other in (ahead, behind):
        pl.semaphore_signal(barrier, inc=1, device_id=(energy, other), device_id_type=MESH)
    for hop in range(1, energies):
        other = lax.rem(energy + hop, energies)
        pl.semaphore_signal(barrier, inc=1, device_id=(other, place), device_id_type=MESH)

    def pass_on(chunk):
        return pltpu.make_async_remote_copy(
            src_ref=wave_out.at[chunk],
            dst_ref=wave_in.at[chunk],
            send_sem=send_sem.at[chunk],
            recv_sem=recv_sem.at[chunk],
            device_id=(energy, ahead),
            device_id_type=MESH,
        )

    smalls[0].wait()
    smalls[1].wait()
    smalls[2].wait()

    tile_row = lax.broadcasted_iota(jnp.int32, (tiles, orbitals), 0)
    column = lax.broadcasted_iota(jnp.int32, (tiles, orbitals), 1)
    offset = column - tile_row * tile
    spread = jnp.where(jnp.logical_and(offset >= 0, offset < tile), 1.0, 0.0).astype(jnp.bfloat16)

    def used_coupling(block):
        mask = dot(pattern[block].astype(jnp.float32).astype(jnp.bfloat16), spread)
        used = coupling[block].reshape(tiles, tile, orbitals) * mask[:, None, :]
        return used.reshape(orbitals, orbitals)

    def green_parts(block):
        return split(green[block].reshape(2 * orbitals, orbitals))

    @pl.when(place == last)
    def _():
        for part in range(2):
            rows = injection[part].T.reshape(chunks, ROWS, orbitals)
            wave_in[:, part * ROWS : (part + 1) * ROWS, :] = rows
        wave_out[...] = wave_in[...]

        def direct(index, carry):
            block = blocks - 1 - index
            for copy in load(block):
                copy.wait()
            wave = wave_out[...].reshape(chunks * 2 * ROWS, orbitals)
            mixed = narrow_product(wave, *split(used_coupling(block)), NT)
            moved = combine(narrow_product(mixed, *green_parts(block), NT), chunks, orbitals)
            wave_out[...] = moved.reshape(chunks, 2 * ROWS, orbitals)
            return carry

        lax.fori_loop(0, blocks, direct, 0)
        pl.semaphore_wait(barrier, energies + 1)
        for chunk in range(chunks):
            pass_on(chunk).start()

    def propagator(index, carry):
        block = blocks - 1 - index

        @pl.when(place < last)
        def _():
            for copy in load(block):
                copy.wait()

        turned = split(used_coupling(block).T)
        value = product(*turned, *green_parts(block), NT)
        parts = split(value)
        high[block] = parts[0]
        low[block] = parts[1]
        return carry

    lax.fori_loop(0, blocks, propagator, 0)

    full = last - 3

    @pl.when(place <= full)
    def _():
        def compose(index, carry):
            first = jnp.where(index == 2, 4, 3 - 2 * index)
            second = jnp.where(index == 2, 5, 2 - 2 * index)
            target = 4 + index
            right = (high[second], low[second])
            real_rows = product(high[first, :, :orbitals], low[first, :, :orbitals], *right)
            imag_rows = product(high[first, :, orbitals:], low[first, :, orbitals:], *right)
            real_part = split(real_rows[:, :orbitals] - imag_rows[:, orbitals:])
            high[target, :, :orbitals] = real_part[0]
            low[target, :, :orbitals] = real_part[1]
            imag_part = split(real_rows[:, orbitals:] + imag_rows[:, :orbitals])
            high[target, :, orbitals:] = imag_part[0]
            low[target, :, orbitals:] = imag_part[1]
            return carry

        lax.fori_loop(0, 3, compose, 0)

    @pl.when(place < last)
    def _():
        pl.semaphore_wait(barrier, energies + 1)

    half = chunks // 2

    @pl.when(jnp.logical_and(place < last, place > full))
    def _():
        for start in (0, half):
            for chunk in range(start, start + half):
                pass_on(chunk).wait_recv()
            wave = wave_in[start : start + half].reshape(half * 2 * ROWS, orbitals)
            for block in reversed(range(blocks)):
                wave = combine(narrow_product(wave, high[block], low[block]), half, orbitals)
            wave_out[start : start + half] = wave.reshape(half, 2 * ROWS, orbitals)
            for chunk in range(start, start + half):
                pass_on(chunk).start()

    @pl.when(jnp.logical_and(place > 0, place <= full))
    def _():
        def hop(chunk, carry):
            pass_on(chunk).wait_recv()
            wave_out[chunk] = combine(narrow_product(wave_in[chunk], high[6], low[6]), 1, orbitals)
            pass_on(chunk).start()
            return carry

        lax.fori_loop(0, chunks, hop, 0)

    @pl.when(place == 0)
    def _():
        for chunk in range(chunks):
            pass_on(chunk).wait_recv()

    def own(index, wave):
        block = blocks - 1 - index
        wave = combine(narrow_product(wave, high[block], low[block]), chunks, orbitals)
        charge = jnp.sum(wave * wave, axis=0, keepdims=True) * (weights[0] / (modes * energies))
        width = orbitals // energies
        for target in range(energies):
            piece = charge[:, target * width : (target + 1) * width]
            part_out[target, pl.ds(block, 1), :width] = piece
        return wave

    lax.fori_loop(0, blocks, own, wave_in[...].reshape(chunks * 2 * ROWS, orbitals))

    def give(hop):
        other = lax.rem(energy + hop, energies)
        return pltpu.make_async_remote_copy(
            src_ref=part_out.at[other],
            dst_ref=part_in.at[hop],
            send_sem=part_send_sem.at[hop],
            recv_sem=part_recv_sem.at[hop],
            device_id=(other, place),
            device_id_type=MESH,
        )

    for hop in range(1, energies):
        give(hop).start()
    total = part_out[energy]
    for hop in range(1, energies):
        give(hop).wait_recv()
        total = total + part_in[hop]
    out_ref[...] = total[:blocks, : orbitals // energies]
    for hop in range(1, energies):
        give(hop).wait_send()

    @pl.when(place > 0)
    def _():
        for chunk in range(chunks):
            pass_on(chunk).wait_send()


def shards(places, energies, green_left, coupling, pattern, injection, weights):
    blocks, orbitals, _ = coupling.shape
    tiles = pattern.shape[1]
    modes = injection.shape[3]
    chunks = modes // ROWS
    sizes = (energies, places, blocks, orbitals, tiles, modes)
    anywhere = pl.BlockSpec(memory_space=pl.ANY)
    return pl.pallas_call(
        functools.partial(kernel, sizes),
        out_shape=jax.ShapeDtypeStruct((blocks, orbitals // energies), jnp.float32),
        in_specs=[anywhere] * 5,
        out_specs=pl.BlockSpec(memory_space=pltpu.VMEM),
        scratch_shapes=[
            pltpu.VMEM((blocks, 2, orbitals, orbitals), jnp.float32),
            pltpu.VMEM((blocks, orbitals, orbitals), jnp.float32),
            pltpu.VMEM(pattern.shape, jnp.int32),
            pltpu.VMEM((2, orbitals, modes), jnp.float32),
            pltpu.SMEM((1,), jnp.float32),
            pltpu.VMEM((7, orbitals, 2 * orbitals), jnp.bfloat16),
            pltpu.VMEM((7, orbitals, 2 * orbitals), jnp.bfloat16),
            pltpu.VMEM((chunks, 2 * ROWS, orbitals), jnp.float32),
            pltpu.VMEM((chunks, 2 * ROWS, orbitals), jnp.float32),
            pltpu.VMEM((energies, 8, 128), jnp.float32),
            pltpu.VMEM((energies, 8, 128), jnp.float32),
            pltpu.SemaphoreType.DMA((2, blocks)),
            pltpu.SemaphoreType.DMA((3,)),
            pltpu.SemaphoreType.DMA((chunks,)),
            pltpu.SemaphoreType.DMA((chunks,)),
            pltpu.SemaphoreType.DMA((energies,)),
            pltpu.SemaphoreType.DMA((energies,)),
        ],
        compiler_params=pltpu.CompilerParams(
            collective_id=0, has_side_effects=True, vmem_limit_bytes=56 * 1024 * 1024
        ),
    )(green_left, coupling, pattern, injection, weights)


def solution(mesh):
    placed = (
        P("energy", "length", None, None, None),
        P("length", None, None),
        P("length", None, None),
        P("energy", None, None, None),
        P("energy"),
    )
    return jax.shard_map(
        functools.partial(shards, mesh.shape["length"], mesh.shape["energy"]),
        mesh=mesh,
        in_specs=placed,
        out_specs=P("length", "energy"),
        check_vma=False,
    )
```

```python
import functools

import jax
import jax.numpy as jnp
from jax import lax
from jax.experimental import pallas as pl
from jax.experimental.pallas import tpu as pltpu
from jax.sharding import PartitionSpec as P

MESH = pl.DeviceIdType.MESH
NN = (((1,), (0,)), ((), ()))
NT = (((1,), (1,)), ((), ()))
ROWS = 4


def split(value):
    high = value.astype(jnp.bfloat16)
    return high, (value - high.astype(jnp.float32)).astype(jnp.bfloat16)


def dot(left, right, dims=NN):
    return lax.dot_general(left, right, dims, preferred_element_type=jnp.float32)


def product(left_high, left_low, right_high, right_low, dims=NN):
    return dot(left_high, right_high, dims) + dot(left_high, right_low, dims) + dot(left_low, right_high, dims)


def narrow_product(wave, right_high, right_low, dims=NN):
    rows = wave.shape[0]
    high = wave.astype(jnp.bfloat16)
    kept = high.astype(jnp.float32)
    stacked = jnp.concatenate([kept, wave - kept], axis=0).astype(jnp.bfloat16)
    both = dot(stacked, right_high, dims)
    return both[:rows] + both[rows:] + dot(high, right_low, dims)


def combine(mixed, orbitals):
    mixed = mixed.reshape(-1, 2 * ROWS, 2 * orbitals)
    row = lax.broadcasted_iota(jnp.int32, (1, 2 * ROWS, orbitals), 1)
    turned = pltpu.roll(mixed[:, :, orbitals:], ROWS, 1)
    moved = mixed[:, :, :orbitals] + jnp.where(row < ROWS, -turned, turned)
    return moved.reshape(-1, orbitals)


def kernel(
    sizes,
    green_hbm,
    coupling_hbm,
    pattern_hbm,
    injection_hbm,
    weights_hbm,
    out_ref,
    green,
    coupling,
    pattern,
    injection,
    weights,
    high,
    low,
    waves,
    wave_out,
    swapped_in,
    part_out,
    part_in,
    charge,
    load_sem,
    small_sem,
    send_sem,
    recv_sem,
    part_send_sem,
    part_recv_sem,
    forward_send_sem,
    forward_recv_sem,
    swap_send_sem,
    swap_recv_sem,
):
    energies, places, blocks, orbitals, tiles, modes = sizes
    chunks = modes // ROWS
    tile = orbitals // tiles
    energy = lax.axis_index("energy")
    place = lax.axis_index("length")
    last = places - 1
    full = last - 2
    wave_in = waves.at[0]
    sibling = energy + 1 - 2 * lax.rem(energy, 2)

    def swaps(where):
        inside = jnp.logical_and(where > 0, where < full)
        return jnp.logical_and(inside, lax.rem(full + 1 - where, 2) == 0)

    swapped = swaps(place)
    sends_to = jnp.where(swapped != swaps(place - 1), sibling, energy)
    sent_by = jnp.where(swapped != swaps(place + 1), sibling, energy)

    def load(block):
        return (
            pltpu.make_async_copy(coupling_hbm.at[block], coupling.at[block], load_sem.at[0, block]),
            pltpu.make_async_copy(green_hbm.at[0, block], green.at[block], load_sem.at[1, block]),
        )

    smalls = (
        pltpu.make_async_copy(pattern_hbm, pattern, small_sem.at[0]),
        pltpu.make_async_copy(injection_hbm.at[0], injection, small_sem.at[1]),
        pltpu.make_async_copy(weights_hbm, weights, small_sem.at[2]),
    )
    smalls[0].start()
    smalls[1].start()
    for copy in load(blocks - 1):
        copy.start()
    smalls[2].start()

    barrier = pltpu.get_barrier_semaphore()
    ahead = lax.rem(place + last, places)
    behind = lax.rem(place + 1, places)
    pl.semaphore_signal(barrier, inc=1, device_id=(sends_to, ahead), device_id_type=MESH)
    pl.semaphore_signal(barrier, inc=1, device_id=(sent_by, behind), device_id_type=MESH)
    for hop in range(1, energies):
        other = lax.rem(energy + hop, energies)
        pl.semaphore_signal(barrier, inc=1, device_id=(other, place), device_id_type=MESH)

    def pass_on(chunk):
        return pltpu.make_async_remote_copy(
            src_ref=wave_out.at[chunk],
            dst_ref=wave_in.at[chunk],
            send_sem=send_sem.at[chunk],
            recv_sem=recv_sem.at[chunk],
            device_id=(sends_to, ahead),
            device_id_type=MESH,
        )

    def forward(chunk):
        return pltpu.make_async_remote_copy(
            src_ref=waves.at[0, chunk],
            dst_ref=waves.at[1, chunk],
            send_sem=forward_send_sem.at[chunk],
            recv_sem=forward_recv_sem.at[chunk],
            device_id=(sibling, place),
            device_id_type=MESH,
        )

    def swap(part):
        return pltpu.make_async_remote_copy(
            src_ref=green.at[0, part],
            dst_ref=swapped_in.at[part],
            send_sem=swap_send_sem.at[part],
            recv_sem=swap_recv_sem.at[part],
            device_id=(sibling, place),
            device_id_type=MESH,
        )

    def arrive(block):
        for copy in load(block):
            copy.wait()

        @pl.when(block > 1)
        def _():
            for copy in load(block - 2):
                copy.start()

    smalls[0].wait()
    smalls[1].wait()
    for copy in load(blocks - 2):
        copy.start()

    tile_row = lax.broadcasted_iota(jnp.int32, (tiles, orbitals), 0)
    column = lax.broadcasted_iota(jnp.int32, (tiles, orbitals), 1)
    offset = column - tile_row * tile
    spread = jnp.where(jnp.logical_and(offset >= 0, offset < tile), 1.0, 0.0).astype(jnp.bfloat16)

    def used_coupling(block):
        mask = dot(pattern[block].astype(jnp.float32).astype(jnp.bfloat16), spread)
        used = coupling[block].reshape(tiles, tile, orbitals) * mask[:, None, :]
        return used.reshape(orbitals, orbitals)

    def green_parts(block):
        return split(green[block].reshape(2 * orbitals, orbitals))

    @pl.when(place == last)
    def _():
        for chunk in range(chunks):
            for part in range(2):
                rows = injection[part, chunk * ROWS : (chunk + 1) * ROWS, :]
                wave_in[chunk, part * ROWS : (part + 1) * ROWS, :] = rows
        wave = wave_in[...].reshape(chunks * 2 * ROWS, orbitals)
        for block in reversed(range(blocks)):
            arrive(block)
            mixed = narrow_product(wave, *split(used_coupling(block)), NT)
            wave = combine(narrow_product(mixed, *green_parts(block), NT), orbitals)
        wave_out[...] = wave.reshape(chunks, 2 * ROWS, orbitals)
        pl.semaphore_wait(barrier, energies + 1)
        for chunk in range(chunks):
            pass_on(chunk).start()

    def propagator(index, carry):
        block = blocks - 1 - index

        @pl.when(place < last)
        def _():
            arrive(block)

        turned = split(used_coupling(block).T)
        value = product(*turned, *green_parts(block), NT)
        parts = split(value)
        high[block] = parts[0]
        low[block] = parts[1]
        return carry

    lax.fori_loop(0, blocks, propagator, 0)

    @pl.when(place <= full)
    def _():
        def compose(index, carry):
            first = jnp.where(index >= 2, 4, 3 - 2 * index)
            second = jnp.where(index >= 2, jnp.where(index == 2, 5, 1), 2 - 2 * index)
            target = jnp.where(index == 3, 5, 4 + index)
            right = (high[second], low[second])
            real_rows = product(high[first, :, :orbitals], low[first, :, :orbitals], *right)
            imag_rows = product(high[first, :, orbitals:], low[first, :, orbitals:], *right)
            real_part = split(real_rows[:, :orbitals] - imag_rows[:, orbitals:])
            high[target, :, :orbitals] = real_part[0]
            low[target, :, :orbitals] = real_part[1]
            imag_part = split(real_rows[:, orbitals:] + imag_rows[:, :orbitals])
            high[target, :, orbitals:] = imag_part[0]
            low[target, :, orbitals:] = imag_part[1]
            return carry

        lax.fori_loop(0, jnp.where(place <= 1, 4, 3), compose, 0)

    @pl.when(place < last)
    def _():
        pl.semaphore_wait(barrier, energies + 1)

    @pl.when(swapped)
    def _():
        for part in range(2):
            columns = slice(part * orbitals, (part + 1) * orbitals)
            green[0, part] = high[6, :, columns].astype(jnp.float32) + low[6, :, columns].astype(jnp.float32)
            swap(part).start()
        for part in range(2):
            columns = slice(part * orbitals, (part + 1) * orbitals)
            swap(part).wait_recv()
            parts = split(swapped_in[part])
            high[6, :, columns] = parts[0]
            low[6, :, columns] = parts[1]

    half = chunks // 2

    def half_hop(maps):
        for start in (0, half):
            for chunk in range(start, start + half):
                pass_on(chunk).wait_recv()
            wave = wave_in[start : start + half].reshape(half * 2 * ROWS, orbitals)
            for block in maps:
                wave = combine(narrow_product(wave, high[block], low[block]), orbitals)
            wave_out[start : start + half] = wave.reshape(half, 2 * ROWS, orbitals)
            for chunk in range(start, start + half):
                pass_on(chunk).start()

    @pl.when(jnp.logical_and(place < last, place > full))
    def _():
        half_hop(tuple(reversed(range(blocks))))

    @pl.when(place == full)
    def _():
        half_hop((6,))

    @pl.when(jnp.logical_and(place > 0, place < full))
    def _():
        def hop(chunk, carry):
            pass_on(chunk).wait_recv()
            wave_out[chunk] = combine(narrow_product(wave_in[chunk], high[6], low[6]), orbitals)
            pass_on(chunk).start()

            @pl.when(swapped)
            def _():
                forward(chunk).start()

            return carry

        lax.fori_loop(0, chunks, hop, 0, unroll=True)

    smalls[2].wait()
    factor = weights[0] / (modes * energies)

    def density(wave):
        return jnp.sum(wave * wave, axis=0, keepdims=True) * factor

    def own(part, carry):
        @pl.when(swapped)
        def _():
            for chunk in range(half):
                forward(part * half + chunk).wait_recv()

        wave = waves[jnp.where(swapped, 1, 0), pl.ds(part * half, half)].reshape(half * 2 * ROWS, orbitals)
        for block in reversed(range(blocks)):
            wave = combine(narrow_product(wave, high[block], low[block]), orbitals)
            charge[part, block : block + 1, :] = density(wave)
        return carry

    def own_at_end(part, carry):
        @pl.when(place == 0)
        def _():
            for chunk in range(half):
                pass_on(part * half + chunk).wait_recv()

        wave = waves[0, pl.ds(part * half, half)].reshape(half * 2 * ROWS, orbitals)
        for block in range(blocks):
            slot = 6 - block
            moved = combine(narrow_product(wave, high[slot], low[slot]), orbitals)
            charge[part, block : block + 1, :] = density(moved)
        return carry

    @pl.when(place > 1)
    def _():
        lax.fori_loop(0, 2, own, 0)

    @pl.when(place <= 1)
    def _():
        lax.fori_loop(0, 2, own_at_end, 0)

    width = orbitals // energies
    summed = charge[0] + charge[1]
    for target in range(energies):
        part_out[target, :blocks, :width] = summed[:, target * width : (target + 1) * width]

    def give(hop):
        other = lax.rem(energy + hop, energies)
        return pltpu.make_async_remote_copy(
            src_ref=part_out.at[other],
            dst_ref=part_in.at[hop],
            send_sem=part_send_sem.at[hop],
            recv_sem=part_recv_sem.at[hop],
            device_id=(other, place),
            device_id_type=MESH,
        )

    for hop in range(1, energies):
        give(hop).start()
    total = part_out[energy]
    for hop in range(1, energies):
        give(hop).wait_recv()
        total = total + part_in[hop]
    out_ref[...] = total[:blocks, : orbitals // energies]
    for hop in range(1, energies):
        give(hop).wait_send()

    @pl.when(place > 0)
    def _():
        for chunk in range(chunks):
            pass_on(chunk).wait_send()

    @pl.when(swapped)
    def _():
        for chunk in range(chunks):
            forward(chunk).wait_send()
        for part in range(2):
            swap(part).wait_send()


def shards(places, energies, green_left, coupling, pattern, injection, weights):
    blocks, orbitals, _ = coupling.shape
    tiles = pattern.shape[1]
    modes = injection.shape[3]
    chunks = modes // ROWS
    sizes = (energies, places, blocks, orbitals, tiles, modes)
    return pl.pallas_call(
        functools.partial(kernel, sizes),
        out_shape=pltpu.VMEM((blocks, orbitals // energies), jnp.float32),
        in_specs=[pl.BlockSpec(memory_space=pltpu.HBM)] * 5,
        out_specs=pl.BlockSpec(memory_space=pltpu.VMEM),
        scratch_shapes=[
            pltpu.VMEM((blocks, 2, orbitals, orbitals), jnp.float32),
            pltpu.VMEM((blocks, orbitals, orbitals), jnp.float32),
            pltpu.VMEM(pattern.shape, jnp.int32),
            pltpu.VMEM((2, modes, orbitals), jnp.float32),
            pltpu.SMEM((1,), jnp.float32),
            pltpu.VMEM((7, orbitals, 2 * orbitals), jnp.bfloat16),
            pltpu.VMEM((7, orbitals, 2 * orbitals), jnp.bfloat16),
            pltpu.VMEM((2, chunks, 2 * ROWS, orbitals), jnp.float32),
            pltpu.VMEM((chunks, 2 * ROWS, orbitals), jnp.float32),
            pltpu.VMEM((2, orbitals, orbitals), jnp.float32),
            pltpu.VMEM((energies, 8, 128), jnp.float32),
            pltpu.VMEM((energies, 8, 128), jnp.float32),
            pltpu.VMEM((2, blocks, orbitals), jnp.float32),
            pltpu.SemaphoreType.DMA((2, blocks)),
            pltpu.SemaphoreType.DMA((3,)),
            pltpu.SemaphoreType.DMA((chunks,)),
            pltpu.SemaphoreType.DMA((chunks,)),
            pltpu.SemaphoreType.DMA((energies,)),
            pltpu.SemaphoreType.DMA((energies,)),
            pltpu.SemaphoreType.DMA((chunks,)),
            pltpu.SemaphoreType.DMA((chunks,)),
            pltpu.SemaphoreType.DMA((2,)),
            pltpu.SemaphoreType.DMA((2,)),
        ],
        compiler_params=pltpu.CompilerParams(
            collective_id=0, has_side_effects=True, vmem_limit_bytes=56 * 1024 * 1024
        ),
    )(green_left, coupling, pattern, jnp.swapaxes(injection, 2, 3), weights)


def solution(mesh):
    placed = (
        P("energy", "length", None, None, None),
        P("length", None, None),
        P("length", None, None),
        P("energy", None, None, None),
        P("energy"),
    )
    return jax.shard_map(
        functools.partial(shards, mesh.shape["length"], mesh.shape["energy"]),
        mesh=mesh,
        in_specs=placed,
        out_specs=P("length", "energy"),
        check_vma=False,
    )
```

```python
import functools

import jax
import jax.numpy as jnp
from jax import lax
from jax.experimental import pallas as pl
from jax.experimental.pallas import tpu as pltpu
from jax.sharding import PartitionSpec as P

MESH = pl.DeviceIdType.MESH
NN = (((1,), (0,)), ((), ()))
NT = (((1,), (1,)), ((), ()))
ROWS = 4


def split(value):
    high = value.astype(jnp.bfloat16)
    return high, (value - high.astype(jnp.float32)).astype(jnp.bfloat16)


def dot(left, right, dims=NN):
    return lax.dot_general(left, right, dims, preferred_element_type=jnp.float32)


def product(left_high, left_low, right_high, right_low, dims=NN):
    return dot(left_high, right_high, dims) + dot(left_high, right_low, dims) + dot(left_low, right_high, dims)


def narrow_product(wave, right_high, right_low, dims=NN):
    rows = wave.shape[0]
    high = wave.astype(jnp.bfloat16)
    kept = high.astype(jnp.float32)
    stacked = jnp.concatenate([kept, wave - kept], axis=0).astype(jnp.bfloat16)
    both = dot(stacked, right_high, dims)
    return both[:rows] + both[rows:] + dot(high, right_low, dims)


def combine(mixed, orbitals):
    mixed = mixed.reshape(-1, 2 * ROWS, 2 * orbitals)
    row = lax.broadcasted_iota(jnp.int32, (1, 2 * ROWS, orbitals), 1)
    turned = pltpu.roll(mixed[:, :, orbitals:], ROWS, 1)
    moved = mixed[:, :, :orbitals] + jnp.where(row < ROWS, -turned, turned)
    return moved.reshape(-1, orbitals)


def kernel(
    sizes,
    green_hbm,
    coupling_hbm,
    pattern_hbm,
    injection_hbm,
    weights_hbm,
    out_ref,
    green,
    coupling,
    pattern,
    injection,
    weights,
    high,
    low,
    waves,
    wave_out,
    swapped_in,
    part_out,
    part_in,
    charge,
    load_sem,
    small_sem,
    send_sem,
    recv_sem,
    part_send_sem,
    part_recv_sem,
    forward_send_sem,
    forward_recv_sem,
    swap_send_sem,
    swap_recv_sem,
):
    energies, places, blocks, orbitals, tiles, modes = sizes
    chunks = modes // ROWS
    tile = orbitals // tiles
    energy = lax.axis_index("energy")
    place = lax.axis_index("length")
    last = places - 1
    full = last - 2
    wave_in = waves.at[0]
    sibling = energy + 1 - 2 * lax.rem(energy, 2)

    def swaps(where):
        inside = jnp.logical_and(where > 0, where < full)
        return jnp.logical_and(inside, lax.rem(full + 1 - where, 2) == 0)

    swapped = swaps(place)
    sends_to = jnp.where(swapped != swaps(place - 1), sibling, energy)
    sent_by = jnp.where(swapped != swaps(place + 1), sibling, energy)

    def load(block, kind):
        if kind == 0:
            return pltpu.make_async_copy(coupling_hbm.at[block], coupling.at[block], load_sem.at[0, block])
        return pltpu.make_async_copy(green_hbm.at[0, block], green.at[block], load_sem.at[1, block])

    smalls = (
        pltpu.make_async_copy(pattern_hbm, pattern, small_sem.at[0]),
        pltpu.make_async_copy(injection_hbm.at[0], injection, small_sem.at[1]),
        pltpu.make_async_copy(weights_hbm, weights, small_sem.at[2]),
    )
    smalls[0].start()
    smalls[1].start()
    for kind in range(2):
        load(blocks - 1, kind).start()
    smalls[2].start()

    barrier = pltpu.get_barrier_semaphore()
    ahead = lax.rem(place + last, places)
    behind = lax.rem(place + 1, places)
    pl.semaphore_signal(barrier, inc=1, device_id=(sends_to, ahead), device_id_type=MESH)
    pl.semaphore_signal(barrier, inc=1, device_id=(sent_by, behind), device_id_type=MESH)
    for hop in range(1, energies):
        other = lax.rem(energy + hop, energies)
        pl.semaphore_signal(barrier, inc=1, device_id=(other, place), device_id_type=MESH)

    def pass_on(chunk):
        return pltpu.make_async_remote_copy(
            src_ref=wave_out.at[chunk],
            dst_ref=wave_in.at[chunk],
            send_sem=send_sem.at[chunk],
            recv_sem=recv_sem.at[chunk],
            device_id=(sends_to, ahead),
            device_id_type=MESH,
        )

    def forward(chunk):
        return pltpu.make_async_remote_copy(
            src_ref=waves.at[0, chunk],
            dst_ref=waves.at[1, chunk],
            send_sem=forward_send_sem.at[chunk],
            recv_sem=forward_recv_sem.at[chunk],
            device_id=(sibling, place),
            device_id_type=MESH,
        )

    def swap(part):
        return pltpu.make_async_remote_copy(
            src_ref=green.at[0, part],
            dst_ref=swapped_in.at[part],
            send_sem=swap_send_sem.at[part],
            recv_sem=swap_recv_sem.at[part],
            device_id=(sibling, place),
            device_id_type=MESH,
        )

    def arrive(block, kind):
        load(block, kind).wait()

        @pl.when(block > 1)
        def _():
            load(block - 2, kind).start()

    smalls[0].wait()
    smalls[1].wait()
    for kind in range(2):
        load(blocks - 2, kind).start()

    tile_row = lax.broadcasted_iota(jnp.int32, (tiles, orbitals), 0)
    column = lax.broadcasted_iota(jnp.int32, (tiles, orbitals), 1)
    offset = column - tile_row * tile
    spread = jnp.where(jnp.logical_and(offset >= 0, offset < tile), 1.0, 0.0).astype(jnp.bfloat16)

    def used_coupling(block):
        mask = dot(pattern[block].astype(jnp.float32).astype(jnp.bfloat16), spread)
        used = coupling[block].reshape(tiles, tile, orbitals) * mask[:, None, :]
        return used.reshape(orbitals, orbitals)

    def green_parts(block):
        return split(green[block].reshape(2 * orbitals, orbitals))

    @pl.when(place == last)
    def _():
        for chunk in range(chunks):
            for part in range(2):
                rows = injection[part, chunk * ROWS : (chunk + 1) * ROWS, :]
                wave_in[chunk, part * ROWS : (part + 1) * ROWS, :] = rows
        wave = wave_in[...].reshape(chunks * 2 * ROWS, orbitals)
        for block in reversed(range(blocks)):
            arrive(block, 0)
            mixed = narrow_product(wave, *split(used_coupling(block)), NT)
            arrive(block, 1)
            wave = combine(narrow_product(mixed, *green_parts(block), NT), orbitals)
        wave_out[...] = wave.reshape(chunks, 2 * ROWS, orbitals)
        pl.semaphore_wait(barrier, energies + 1)
        for chunk in range(chunks):
            pass_on(chunk).start()

    def propagator(index, carry):
        block = blocks - 1 - index

        @pl.when(place < last)
        def _():
            arrive(block, 0)
            arrive(block, 1)

        turned = split(used_coupling(block).T)
        value = product(*turned, *green_parts(block), NT)
        parts = split(value)
        high[block] = parts[0]
        low[block] = parts[1]
        return carry

    lax.fori_loop(0, blocks, propagator, 0)

    @pl.when(place <= full)
    def _():
        def compose(index, carry):
            first = jnp.where(index >= 2, 4, 3 - 2 * index)
            second = jnp.where(index >= 2, jnp.where(index == 2, 5, 1), 2 - 2 * index)
            target = jnp.where(index == 3, 5, 4 + index)
            def sides(slot):
                return [
                    (high[slot, :, side * orbitals : (side + 1) * orbitals], low[slot, :, side * orbitals : (side + 1) * orbitals])
                    for side in range(2)
                ]

            def summed_sides(parts):
                whole = [part[0].astype(jnp.float32) + part[1].astype(jnp.float32) for part in parts]
                return split(whole[0] + whole[1])

            left, right = sides(first), sides(second)
            reals = product(*left[0], *right[0])
            imags = product(*left[1], *right[1])
            crossed = product(*summed_sides(left), *summed_sides(right))
            real_part = split(reals - imags)
            high[target, :, :orbitals] = real_part[0]
            low[target, :, :orbitals] = real_part[1]
            imag_part = split(crossed - reals - imags)
            high[target, :, orbitals:] = imag_part[0]
            low[target, :, orbitals:] = imag_part[1]
            return carry

        lax.fori_loop(0, jnp.where(place <= 1, 4, 3), compose, 0)

    @pl.when(place < last)
    def _():
        pl.semaphore_wait(barrier, energies + 1)

    @pl.when(swapped)
    def _():
        for part in range(2):
            columns = slice(part * orbitals, (part + 1) * orbitals)
            green[0, part] = high[6, :, columns].astype(jnp.float32) + low[6, :, columns].astype(jnp.float32)
            swap(part).start()
        for part in range(2):
            columns = slice(part * orbitals, (part + 1) * orbitals)
            swap(part).wait_recv()
            parts = split(swapped_in[part])
            high[6, :, columns] = parts[0]
            low[6, :, columns] = parts[1]

    half = chunks // 2

    def half_hop(maps):
        for start in (0, half):
            for chunk in range(start, start + half):
                pass_on(chunk).wait_recv()
            wave = wave_in[start : start + half].reshape(half * 2 * ROWS, orbitals)
            for block in maps:
                wave = combine(narrow_product(wave, high[block], low[block]), orbitals)
            wave_out[start : start + half] = wave.reshape(half, 2 * ROWS, orbitals)
            for chunk in range(start, start + half):
                pass_on(chunk).start()

    @pl.when(jnp.logical_and(place < last, place > full))
    def _():
        half_hop(tuple(reversed(range(blocks))))

    def hops(forwards):
        for chunk in range(chunks):
            pass_on(chunk).wait_recv()
            wave_out[chunk] = combine(narrow_product(wave_in[chunk], high[6], low[6]), orbitals)
            pass_on(chunk).start()
            if forwards:
                forward(chunk).start()

    @pl.when(swapped)
    def _():
        hops(True)

    @pl.when(jnp.logical_and(jnp.logical_and(place > 0, place <= full), jnp.logical_not(swapped)))
    def _():
        hops(False)

    smalls[2].wait()
    factor = weights[0] / (modes * energies)

    def density(wave):
        return jnp.sum(wave * wave, axis=0, keepdims=True) * factor

    def own(part, carry):
        @pl.when(swapped)
        def _():
            for chunk in range(half):
                forward(part * half + chunk).wait_recv()

        wave = waves[jnp.where(swapped, 1, 0), pl.ds(part * half, half)].reshape(half * 2 * ROWS, orbitals)
        for block in reversed(range(blocks)):
            wave = combine(narrow_product(wave, high[block], low[block]), orbitals)
            charge[part, block : block + 1, :] = density(wave)
        return carry

    def own_at_end(part, carry):
        @pl.when(place == 0)
        def _():
            for chunk in range(half):
                pass_on(part * half + chunk).wait_recv()

        wave = waves[0, pl.ds(part * half, half)].reshape(half * 2 * ROWS, orbitals)
        for block in range(blocks):
            slot = 6 - block
            moved = combine(narrow_product(wave, high[slot], low[slot]), orbitals)
            charge[part, block : block + 1, :] = density(moved)
        return carry

    @pl.when(place > 1)
    def _():
        lax.fori_loop(0, 2, own, 0)

    @pl.when(place <= 1)
    def _():
        lax.fori_loop(0, 2, own_at_end, 0)

    width = orbitals // energies
    summed = charge[0] + charge[1]
    for target in range(energies):
        part_out[target, :blocks, :width] = summed[:, target * width : (target + 1) * width]

    def give(hop):
        other = lax.rem(energy + hop, energies)
        return pltpu.make_async_remote_copy(
            src_ref=part_out.at[other],
            dst_ref=part_in.at[hop],
            send_sem=part_send_sem.at[hop],
            recv_sem=part_recv_sem.at[hop],
            device_id=(other, place),
            device_id_type=MESH,
        )

    for hop in range(1, energies):
        give(hop).start()
    total = part_out[energy]
    for hop in range(1, energies):
        give(hop).wait_recv()
        total = total + part_in[hop]
    out_ref[...] = total[:blocks, : orbitals // energies]
    for hop in range(1, energies):
        give(hop).wait_send()

    @pl.when(place > 0)
    def _():
        for chunk in range(chunks):
            pass_on(chunk).wait_send()

    @pl.when(swapped)
    def _():
        for chunk in range(chunks):
            forward(chunk).wait_send()
        for part in range(2):
            swap(part).wait_send()


def shards(places, energies, green_left, coupling, pattern, injection, weights):
    blocks, orbitals, _ = coupling.shape
    tiles = pattern.shape[1]
    modes = injection.shape[3]
    chunks = modes // ROWS
    sizes = (energies, places, blocks, orbitals, tiles, modes)
    return pl.pallas_call(
        functools.partial(kernel, sizes),
        out_shape=pltpu.VMEM((blocks, orbitals // energies), jnp.float32),
        in_specs=[pl.BlockSpec(memory_space=pltpu.HBM)] * 5,
        out_specs=pl.BlockSpec(memory_space=pltpu.VMEM),
        scratch_shapes=[
            pltpu.VMEM((blocks, 2, orbitals, orbitals), jnp.float32),
            pltpu.VMEM((blocks, orbitals, orbitals), jnp.float32),
            pltpu.VMEM(pattern.shape, jnp.int32),
            pltpu.VMEM((2, modes, orbitals), jnp.float32),
            pltpu.SMEM((1,), jnp.float32),
            pltpu.VMEM((7, orbitals, 2 * orbitals), jnp.bfloat16),
            pltpu.VMEM((7, orbitals, 2 * orbitals), jnp.bfloat16),
            pltpu.VMEM((2, chunks, 2 * ROWS, orbitals), jnp.float32),
            pltpu.VMEM((chunks, 2 * ROWS, orbitals), jnp.float32),
            pltpu.VMEM((2, orbitals, orbitals), jnp.float32),
            pltpu.VMEM((energies, 8, 128), jnp.float32),
            pltpu.VMEM((energies, 8, 128), jnp.float32),
            pltpu.VMEM((2, blocks, orbitals), jnp.float32),
            pltpu.SemaphoreType.DMA((2, blocks)),
            pltpu.SemaphoreType.DMA((3,)),
            pltpu.SemaphoreType.DMA((chunks,)),
            pltpu.SemaphoreType.DMA((chunks,)),
            pltpu.SemaphoreType.DMA((energies,)),
            pltpu.SemaphoreType.DMA((energies,)),
            pltpu.SemaphoreType.DMA((chunks,)),
            pltpu.SemaphoreType.DMA((chunks,)),
            pltpu.SemaphoreType.DMA((2,)),
            pltpu.SemaphoreType.DMA((2,)),
        ],
        compiler_params=pltpu.CompilerParams(
            collective_id=0, has_side_effects=True, vmem_limit_bytes=56 * 1024 * 1024
        ),
    )(green_left, coupling, pattern, jnp.swapaxes(injection, 2, 3), weights)


def solution(mesh):
    placed = (
        P("energy", "length", None, None, None),
        P("length", None, None),
        P("length", None, None),
        P("energy", None, None, None),
        P("energy"),
    )
    return jax.shard_map(
        functools.partial(shards, mesh.shape["length"], mesh.shape["energy"]),
        mesh=mesh,
        in_specs=placed,
        out_specs=P("length", "energy"),
        check_vma=False,
    )
```

```python
import functools

import jax
import jax.numpy as jnp
from jax import lax
from jax.experimental import pallas as pl
from jax.experimental.pallas import tpu as pltpu
from jax.sharding import PartitionSpec as P

MESH = pl.DeviceIdType.MESH
NN = (((1,), (0,)), ((), ()))
NT = (((1,), (1,)), ((), ()))
ROWS = 4


def split(value):
    high = value.astype(jnp.bfloat16)
    return high, (value - high.astype(jnp.float32)).astype(jnp.bfloat16)


def dot(left, right, dims=NN):
    return lax.dot_general(left, right, dims, preferred_element_type=jnp.float32)


def product(left_high, left_low, right_high, right_low, dims=NN):
    return dot(left_high, right_high, dims) + dot(left_high, right_low, dims) + dot(left_low, right_high, dims)


def narrow_product(wave, right_high, right_low, dims=NN):
    rows = wave.shape[0]
    high = wave.astype(jnp.bfloat16)
    kept = high.astype(jnp.float32)
    stacked = jnp.concatenate([kept, wave - kept], axis=0).astype(jnp.bfloat16)
    both = dot(stacked, right_high, dims)
    return both[:rows] + both[rows:] + dot(high, right_low, dims)


def combine(mixed, orbitals):
    mixed = mixed.reshape(-1, 2 * ROWS, 2 * orbitals)
    row = lax.broadcasted_iota(jnp.int32, (1, 2 * ROWS, orbitals), 1)
    turned = pltpu.roll(mixed[:, :, orbitals:], ROWS, 1)
    moved = mixed[:, :, :orbitals] + jnp.where(row < ROWS, -turned, turned)
    return moved.reshape(-1, orbitals)


def kernel(
    sizes,
    green_hbm,
    coupling_hbm,
    pattern_hbm,
    injection_hbm,
    weights_hbm,
    out_ref,
    green,
    coupling,
    pattern,
    injection,
    weights,
    high,
    low,
    waves,
    wave_out,
    swapped_in,
    part_out,
    part_in,
    charge,
    load_sem,
    small_sem,
    send_sem,
    recv_sem,
    part_send_sem,
    part_recv_sem,
    forward_send_sem,
    forward_recv_sem,
    swap_send_sem,
    swap_recv_sem,
):
    energies, places, blocks, orbitals, tiles, modes = sizes
    chunks = modes // ROWS
    tile = orbitals // tiles
    energy = lax.axis_index("energy")
    place = lax.axis_index("length")
    last = places - 1
    full = last - 2
    wave_in = waves.at[0]
    sibling = energy + 1 - 2 * lax.rem(energy, 2)

    def swaps(where):
        inside = jnp.logical_and(where > 0, where < full)
        return jnp.logical_and(inside, lax.rem(full + 1 - where, 2) == 0)

    swapped = swaps(place)
    sends_to = jnp.where(swapped != swaps(place - 1), sibling, energy)
    sent_by = jnp.where(swapped != swaps(place + 1), sibling, energy)

    def load(block, kind):
        if kind == 0:
            return pltpu.make_async_copy(coupling_hbm.at[block], coupling.at[block], load_sem.at[0, block])
        return pltpu.make_async_copy(green_hbm.at[0, block], green.at[block], load_sem.at[1, block])

    smalls = (
        pltpu.make_async_copy(pattern_hbm, pattern, small_sem.at[0]),
        pltpu.make_async_copy(injection_hbm.at[0], injection, small_sem.at[1]),
        pltpu.make_async_copy(weights_hbm, weights, small_sem.at[2]),
    )
    smalls[0].start()
    smalls[1].start()
    for kind in range(2):
        load(blocks - 1, kind).start()
    smalls[2].start()

    barrier = pltpu.get_barrier_semaphore()
    ahead = lax.rem(place + last, places)
    behind = lax.rem(place + 1, places)
    pl.semaphore_signal(barrier, inc=1, device_id=(sends_to, ahead), device_id_type=MESH)
    pl.semaphore_signal(barrier, inc=1, device_id=(sent_by, behind), device_id_type=MESH)
    for hop in range(1, energies):
        other = lax.rem(energy + hop, energies)
        pl.semaphore_signal(barrier, inc=1, device_id=(other, place), device_id_type=MESH)

    def pass_on(chunk):
        return pltpu.make_async_remote_copy(
            src_ref=wave_out.at[chunk],
            dst_ref=wave_in.at[chunk],
            send_sem=send_sem.at[chunk],
            recv_sem=recv_sem.at[chunk],
            device_id=(sends_to, ahead),
            device_id_type=MESH,
        )

    def forward(chunk):
        return pltpu.make_async_remote_copy(
            src_ref=waves.at[0, chunk],
            dst_ref=waves.at[1, chunk],
            send_sem=forward_send_sem.at[chunk],
            recv_sem=forward_recv_sem.at[chunk],
            device_id=(sibling, place),
            device_id_type=MESH,
        )

    def swap(part):
        return pltpu.make_async_remote_copy(
            src_ref=green.at[0, part],
            dst_ref=swapped_in.at[part],
            send_sem=swap_send_sem.at[part],
            recv_sem=swap_recv_sem.at[part],
            device_id=(sibling, place),
            device_id_type=MESH,
        )

    def arrive(block, kind):
        load(block, kind).wait()

        @pl.when(block > 1)
        def _():
            load(block - 2, kind).start()

    smalls[0].wait()
    smalls[1].wait()
    for kind in range(2):
        load(blocks - 2, kind).start()

    tile_row = lax.broadcasted_iota(jnp.int32, (tiles, orbitals), 0)
    column = lax.broadcasted_iota(jnp.int32, (tiles, orbitals), 1)
    offset = column - tile_row * tile
    spread = jnp.where(jnp.logical_and(offset >= 0, offset < tile), 1.0, 0.0).astype(jnp.bfloat16)

    def used_coupling(block):
        mask = dot(pattern[block].astype(jnp.float32).astype(jnp.bfloat16), spread)
        used = coupling[block].reshape(tiles, tile, orbitals) * mask[:, None, :]
        return used.reshape(orbitals, orbitals)

    def green_parts(block):
        return split(green[block].reshape(2 * orbitals, orbitals))

    @pl.when(place == last)
    def _():
        for chunk in range(chunks):
            for part in range(2):
                rows = injection[part, chunk * ROWS : (chunk + 1) * ROWS, :]
                wave_in[chunk, part * ROWS : (part + 1) * ROWS, :] = rows
        wave = wave_in[...].reshape(chunks * 2 * ROWS, orbitals)
        for block in reversed(range(1, blocks)):
            arrive(block, 0)
            mixed = narrow_product(wave, *split(used_coupling(block)), NT)
            arrive(block, 1)
            wave = combine(narrow_product(mixed, *green_parts(block), NT), orbitals)
        arrive(0, 0)
        arrive(0, 1)
        pl.semaphore_wait(barrier, energies + 1)
        used, greens = split(used_coupling(0)), green_parts(0)
        rows = modes
        for side in range(2):
            mixed = narrow_product(wave[side * rows : (side + 1) * rows], *used, NT)
            moved = combine(narrow_product(mixed, *greens, NT), orbitals)
            first = side * (chunks // 2)
            wave_out[first : first + chunks // 2] = moved.reshape(chunks // 2, 2 * ROWS, orbitals)
            for chunk in range(first, first + chunks // 2):
                pass_on(chunk).start()

    def propagator(index, carry):
        block = blocks - 1 - index

        @pl.when(place < last)
        def _():
            arrive(block, 0)
            arrive(block, 1)

        turned = split(used_coupling(block).T)
        value = product(*turned, *green_parts(block), NT)
        parts = split(value)
        high[block] = parts[0]
        low[block] = parts[1]
        return carry

    lax.fori_loop(0, blocks, propagator, 0)

    @pl.when(place <= full)
    def _():
        def compose(index, carry):
            first = jnp.where(index >= 2, 4, 3 - 2 * index)
            second = jnp.where(index >= 2, jnp.where(index == 2, 5, 1), 2 - 2 * index)
            target = jnp.where(index == 3, 5, 4 + index)
            def sides(slot):
                return [
                    (high[slot, :, side * orbitals : (side + 1) * orbitals], low[slot, :, side * orbitals : (side + 1) * orbitals])
                    for side in range(2)
                ]

            def summed_sides(parts):
                whole = [part[0].astype(jnp.float32) + part[1].astype(jnp.float32) for part in parts]
                return split(whole[0] + whole[1])

            left, right = sides(first), sides(second)
            reals = product(*left[0], *right[0])
            imags = product(*left[1], *right[1])
            crossed = product(*summed_sides(left), *summed_sides(right))
            real_part = split(reals - imags)
            high[target, :, :orbitals] = real_part[0]
            low[target, :, :orbitals] = real_part[1]
            imag_part = split(crossed - reals - imags)
            high[target, :, orbitals:] = imag_part[0]
            low[target, :, orbitals:] = imag_part[1]
            return carry

        lax.fori_loop(0, jnp.where(place <= 1, 4, 3), compose, 0)

    @pl.when(place < last)
    def _():
        pl.semaphore_wait(barrier, energies + 1)

    @pl.when(swapped)
    def _():
        for part in range(2):
            columns = slice(part * orbitals, (part + 1) * orbitals)
            green[0, part] = high[6, :, columns].astype(jnp.float32) + low[6, :, columns].astype(jnp.float32)
            swap(part).start()
        for part in range(2):
            columns = slice(part * orbitals, (part + 1) * orbitals)
            swap(part).wait_recv()
            parts = split(swapped_in[part])
            high[6, :, columns] = parts[0]
            low[6, :, columns] = parts[1]

    half = chunks // 2

    def half_hop(maps):
        for start in (0, half):
            for chunk in range(start, start + half):
                pass_on(chunk).wait_recv()
            wave = wave_in[start : start + half].reshape(half * 2 * ROWS, orbitals)
            for block in maps:
                wave = combine(narrow_product(wave, high[block], low[block]), orbitals)
            wave_out[start : start + half] = wave.reshape(half, 2 * ROWS, orbitals)
            for chunk in range(start, start + half):
                pass_on(chunk).start()

    @pl.when(jnp.logical_and(place < last, place > full))
    def _():
        half_hop(tuple(reversed(range(blocks))))

    def hops(forwards):
        for chunk in range(chunks):
            pass_on(chunk).wait_recv()
            wave_out[chunk] = combine(narrow_product(wave_in[chunk], high[6], low[6]), orbitals)
            pass_on(chunk).start()
            if forwards and chunk % 4 == 3:
                for earlier in range(chunk - 3, chunk + 1):
                    forward(earlier).start()

    @pl.when(swapped)
    def _():
        hops(True)

    @pl.when(jnp.logical_and(jnp.logical_and(place > 0, place <= full), jnp.logical_not(swapped)))
    def _():
        hops(False)

    smalls[2].wait()
    factor = weights[0] / (modes * energies)

    def density(wave):
        return jnp.sum(wave * wave, axis=0, keepdims=True) * factor

    def own(part, carry):
        @pl.when(swapped)
        def _():
            for chunk in range(half):
                forward(part * half + chunk).wait_recv()

        wave = waves[jnp.where(swapped, 1, 0), pl.ds(part * half, half)].reshape(half * 2 * ROWS, orbitals)
        for block in reversed(range(blocks)):
            wave = combine(narrow_product(wave, high[block], low[block]), orbitals)
            charge[part, block : block + 1, :] = density(wave)
        return carry

    def own_at_end(part, carry):
        @pl.when(place == 0)
        def _():
            for chunk in range(half):
                pass_on(part * half + chunk).wait_recv()

        wave = waves[0, pl.ds(part * half, half)].reshape(half * 2 * ROWS, orbitals)
        for block in range(blocks):
            slot = 6 - block
            moved = combine(narrow_product(wave, high[slot], low[slot]), orbitals)
            charge[part, block : block + 1, :] = density(moved)
        return carry

    @pl.when(place > 1)
    def _():
        lax.fori_loop(0, 2, own, 0)

    @pl.when(place <= 1)
    def _():
        lax.fori_loop(0, 2, own_at_end, 0)

    width = orbitals // energies
    summed = charge[0] + charge[1]
    for target in range(energies):
        part_out[target, :blocks, :width] = summed[:, target * width : (target + 1) * width]

    def give(hop):
        other = lax.rem(energy + hop, energies)
        return pltpu.make_async_remote_copy(
            src_ref=part_out.at[other],
            dst_ref=part_in.at[hop],
            send_sem=part_send_sem.at[hop],
            recv_sem=part_recv_sem.at[hop],
            device_id=(other, place),
            device_id_type=MESH,
        )

    for hop in range(1, energies):
        give(hop).start()
    total = part_out[energy]
    for hop in range(1, energies):
        give(hop).wait_recv()
        total = total + part_in[hop]
    out_ref[...] = total[:blocks, : orbitals // energies]
    for hop in range(1, energies):
        give(hop).wait_send()

    @pl.when(place > 0)
    def _():
        for chunk in range(chunks):
            pass_on(chunk).wait_send()

    @pl.when(swapped)
    def _():
        for chunk in range(chunks):
            forward(chunk).wait_send()
        for part in range(2):
            swap(part).wait_send()


def shards(places, energies, green_left, coupling, pattern, injection, weights):
    blocks, orbitals, _ = coupling.shape
    tiles = pattern.shape[1]
    modes = injection.shape[3]
    chunks = modes // ROWS
    sizes = (energies, places, blocks, orbitals, tiles, modes)
    return pl.pallas_call(
        functools.partial(kernel, sizes),
        out_shape=pltpu.VMEM((blocks, orbitals // energies), jnp.float32),
        in_specs=[pl.BlockSpec(memory_space=pltpu.HBM)] * 5,
        out_specs=pl.BlockSpec(memory_space=pltpu.VMEM),
        scratch_shapes=[
            pltpu.VMEM((blocks, 2, orbitals, orbitals), jnp.float32),
            pltpu.VMEM((blocks, orbitals, orbitals), jnp.float32),
            pltpu.VMEM(pattern.shape, jnp.int32),
            pltpu.VMEM((2, modes, orbitals), jnp.float32),
            pltpu.SMEM((1,), jnp.float32),
            pltpu.VMEM((7, orbitals, 2 * orbitals), jnp.bfloat16),
            pltpu.VMEM((7, orbitals, 2 * orbitals), jnp.bfloat16),
            pltpu.VMEM((2, chunks, 2 * ROWS, orbitals), jnp.float32),
            pltpu.VMEM((chunks, 2 * ROWS, orbitals), jnp.float32),
            pltpu.VMEM((2, orbitals, orbitals), jnp.float32),
            pltpu.VMEM((energies, 8, 128), jnp.float32),
            pltpu.VMEM((energies, 8, 128), jnp.float32),
            pltpu.VMEM((2, blocks, orbitals), jnp.float32),
            pltpu.SemaphoreType.DMA((2, blocks)),
            pltpu.SemaphoreType.DMA((3,)),
            pltpu.SemaphoreType.DMA((chunks,)),
            pltpu.SemaphoreType.DMA((chunks,)),
            pltpu.SemaphoreType.DMA((energies,)),
            pltpu.SemaphoreType.DMA((energies,)),
            pltpu.SemaphoreType.DMA((chunks,)),
            pltpu.SemaphoreType.DMA((chunks,)),
            pltpu.SemaphoreType.DMA((2,)),
            pltpu.SemaphoreType.DMA((2,)),
        ],
        compiler_params=pltpu.CompilerParams(
            collective_id=0, has_side_effects=True, vmem_limit_bytes=56 * 1024 * 1024
        ),
    )(green_left, coupling, pattern, jnp.swapaxes(injection, 2, 3), weights)


def solution(mesh):
    placed = (
        P("energy", "length", None, None, None),
        P("length", None, None),
        P("length", None, None),
        P("energy", None, None, None),
        P("energy"),
    )
    return jax.shard_map(
        functools.partial(shards, mesh.shape["length"], mesh.shape["energy"]),
        mesh=mesh,
        in_specs=placed,
        out_specs=P("length", "energy"),
        check_vma=False,
    )
```

```python
import functools

import jax
import jax.numpy as jnp
from jax import lax
from jax.experimental import pallas as pl
from jax.experimental.pallas import tpu as pltpu
from jax.sharding import PartitionSpec as P

MESH = pl.DeviceIdType.MESH
NN = (((1,), (0,)), ((), ()))
NT = (((1,), (1,)), ((), ()))
ROWS = 4


def split(value):
    high = value.astype(jnp.bfloat16)
    return high, (value - high.astype(jnp.float32)).astype(jnp.bfloat16)


def dot(left, right, dims=NN):
    return lax.dot_general(left, right, dims, preferred_element_type=jnp.float32)


def product(left_high, left_low, right_high, right_low, dims=NN):
    return dot(left_high, right_high, dims) + dot(left_high, right_low, dims) + dot(left_low, right_high, dims)


def narrow_product(wave, right_high, right_low, dims=NN):
    rows = wave.shape[0]
    high = wave.astype(jnp.bfloat16)
    kept = high.astype(jnp.float32)
    stacked = jnp.concatenate([kept, wave - kept], axis=0).astype(jnp.bfloat16)
    both = dot(stacked, right_high, dims)
    return both[:rows] + both[rows:] + dot(high, right_low, dims)


def combine(mixed, orbitals):
    mixed = mixed.reshape(-1, 2 * ROWS, 2 * orbitals)
    row = lax.broadcasted_iota(jnp.int32, (1, 2 * ROWS, orbitals), 1)
    turned = pltpu.roll(mixed[:, :, orbitals:], ROWS, 1)
    moved = mixed[:, :, :orbitals] + jnp.where(row < ROWS, -turned, turned)
    return moved.reshape(-1, orbitals)


def kernel(
    sizes,
    green_hbm,
    coupling_hbm,
    pattern_hbm,
    injection_hbm,
    weights_hbm,
    out_ref,
    green,
    coupling,
    pattern,
    injection,
    weights,
    high,
    low,
    waves,
    wave_out,
    swapped_in,
    part_out,
    part_in,
    charge,
    load_sem,
    small_sem,
    send_sem,
    recv_sem,
    part_send_sem,
    part_recv_sem,
    forward_send_sem,
    forward_recv_sem,
    swap_send_sem,
    swap_recv_sem,
):
    energies, places, blocks, orbitals, tiles, modes = sizes
    chunks = modes // ROWS
    tile = orbitals // tiles
    energy = lax.axis_index("energy")
    place = lax.axis_index("length")
    last = places - 1
    full = last - 2
    wave_in = waves.at[0]
    sibling = energy + 1 - 2 * lax.rem(energy, 2)

    def swaps(where):
        inside = jnp.logical_and(where > 0, where < full)
        return jnp.logical_and(inside, lax.rem(full + 1 - where, 2) == 0)

    swapped = swaps(place)
    sends_to = jnp.where(swapped != swaps(place - 1), sibling, energy)
    sent_by = jnp.where(swapped != swaps(place + 1), sibling, energy)

    def load(block, kind):
        if kind == 0:
            return pltpu.make_async_copy(coupling_hbm.at[block], coupling.at[block], load_sem.at[0, block])
        return pltpu.make_async_copy(green_hbm.at[0, block], green.at[block], load_sem.at[1, block])

    smalls = (
        pltpu.make_async_copy(pattern_hbm, pattern, small_sem.at[0]),
        pltpu.make_async_copy(injection_hbm.at[0], injection, small_sem.at[1]),
        pltpu.make_async_copy(weights_hbm, weights, small_sem.at[2]),
    )
    smalls[0].start()
    smalls[1].start()
    for kind in range(2):
        load(blocks - 1, kind).start()
    smalls[2].start()

    barrier = pltpu.get_barrier_semaphore()
    ahead = lax.rem(place + last, places)
    behind = lax.rem(place + 1, places)
    pl.semaphore_signal(barrier, inc=1, device_id=(sends_to, ahead), device_id_type=MESH)
    pl.semaphore_signal(barrier, inc=1, device_id=(sent_by, behind), device_id_type=MESH)
    for hop in range(1, energies):
        other = lax.rem(energy + hop, energies)
        pl.semaphore_signal(barrier, inc=1, device_id=(other, place), device_id_type=MESH)

    def pass_on(chunk):
        return pltpu.make_async_remote_copy(
            src_ref=wave_out.at[chunk],
            dst_ref=wave_in.at[chunk],
            send_sem=send_sem.at[chunk],
            recv_sem=recv_sem.at[chunk],
            device_id=(sends_to, ahead),
            device_id_type=MESH,
        )

    def forward(chunk):
        return pltpu.make_async_remote_copy(
            src_ref=waves.at[0, chunk],
            dst_ref=waves.at[1, chunk],
            send_sem=forward_send_sem.at[chunk],
            recv_sem=forward_recv_sem.at[chunk],
            device_id=(sibling, place),
            device_id_type=MESH,
        )

    def swap(part):
        return pltpu.make_async_remote_copy(
            src_ref=green.at[0, part],
            dst_ref=swapped_in.at[part],
            send_sem=swap_send_sem.at[part],
            recv_sem=swap_recv_sem.at[part],
            device_id=(sibling, place),
            device_id_type=MESH,
        )

    def arrive(block, kind):
        load(block, kind).wait()

        @pl.when(block > 1)
        def _():
            load(block - 2, kind).start()

    smalls[0].wait()
    smalls[1].wait()
    for kind in range(2):
        load(blocks - 2, kind).start()

    tile_row = lax.broadcasted_iota(jnp.int32, (tiles, orbitals), 0)
    column = lax.broadcasted_iota(jnp.int32, (tiles, orbitals), 1)
    offset = column - tile_row * tile
    spread = jnp.where(jnp.logical_and(offset >= 0, offset < tile), 1.0, 0.0).astype(jnp.bfloat16)

    def used_coupling(block):
        mask = dot(pattern[block].astype(jnp.float32).astype(jnp.bfloat16), spread)
        used = coupling[block].reshape(tiles, tile, orbitals) * mask[:, None, :]
        return used.reshape(orbitals, orbitals)

    def green_parts(block):
        return split(green[block].reshape(2 * orbitals, orbitals))

    @pl.when(place == last)
    def _():
        for chunk in range(chunks):
            for part in range(2):
                rows = injection[part, chunk * ROWS : (chunk + 1) * ROWS, :]
                wave_in[chunk, part * ROWS : (part + 1) * ROWS, :] = rows
        wave = wave_in[...].reshape(chunks * 2 * ROWS, orbitals)
        for block in reversed(range(blocks)):
            arrive(block, 0)
            mixed = narrow_product(wave, *split(used_coupling(block)), NT)
            arrive(block, 1)
            wave = combine(narrow_product(mixed, *green_parts(block), NT), orbitals)
        wave_out[...] = wave.reshape(chunks, 2 * ROWS, orbitals)
        pl.semaphore_wait(barrier, energies + 1)
        for chunk in range(chunks):
            pass_on(chunk).start()

    def propagator(index, carry):
        block = blocks - 1 - index

        @pl.when(place < last)
        def _():
            arrive(block, 0)
            arrive(block, 1)

        turned = split(used_coupling(block).T)
        value = product(*turned, *green_parts(block), NT)
        parts = split(value)
        high[block] = parts[0]
        low[block] = parts[1]
        return carry

    lax.fori_loop(0, blocks, propagator, 0)

    @pl.when(place <= full)
    def _():
        def compose(index, carry):
            first = jnp.where(index >= 2, 4, 3 - 2 * index)
            second = jnp.where(index >= 2, jnp.where(index == 2, 5, 1), 2 - 2 * index)
            target = jnp.where(index == 3, 5, 4 + index)
            def sides(slot):
                return [
                    (high[slot, :, side * orbitals : (side + 1) * orbitals], low[slot, :, side * orbitals : (side + 1) * orbitals])
                    for side in range(2)
                ]

            def summed_sides(parts):
                whole = [part[0].astype(jnp.float32) + part[1].astype(jnp.float32) for part in parts]
                return split(whole[0] + whole[1])

            left, right = sides(first), sides(second)
            reals = product(*left[0], *right[0])
            imags = product(*left[1], *right[1])
            crossed = product(*summed_sides(left), *summed_sides(right))
            real_part = split(reals - imags)
            high[target, :, :orbitals] = real_part[0]
            low[target, :, :orbitals] = real_part[1]
            imag_part = split(crossed - reals - imags)
            high[target, :, orbitals:] = imag_part[0]
            low[target, :, orbitals:] = imag_part[1]
            return carry

        lax.fori_loop(0, jnp.where(place <= 1, 4, 3), compose, 0)

    @pl.when(place < last)
    def _():
        pl.semaphore_wait(barrier, energies + 1)

    @pl.when(swapped)
    def _():
        for part in range(2):
            columns = slice(part * orbitals, (part + 1) * orbitals)
            green[0, part] = high[6, :, columns].astype(jnp.float32) + low[6, :, columns].astype(jnp.float32)
            swap(part).start()
        for part in range(2):
            columns = slice(part * orbitals, (part + 1) * orbitals)
            swap(part).wait_recv()
            parts = split(swapped_in[part])
            high[6, :, columns] = parts[0]
            low[6, :, columns] = parts[1]

    half = chunks // 2

    def half_hop(maps):
        for start in (0, half):
            for chunk in range(start, start + half):
                pass_on(chunk).wait_recv()
            wave = wave_in[start : start + half].reshape(half * 2 * ROWS, orbitals)
            for block in maps:
                wave = combine(narrow_product(wave, high[block], low[block]), orbitals)
            wave_out[start : start + half] = wave.reshape(half, 2 * ROWS, orbitals)
            for chunk in range(start, start + half):
                pass_on(chunk).start()

    @pl.when(jnp.logical_and(place < last, place > full))
    def _():
        half_hop(tuple(reversed(range(blocks))))

    def hops(forwards):
        for chunk in range(chunks):
            pass_on(chunk).wait_recv()
            wave_out[chunk] = combine(narrow_product(wave_in[chunk], high[6], low[6]), orbitals)
            pass_on(chunk).start()
            if forwards:
                forward(chunk).start()

    @pl.when(swapped)
    def _():
        hops(True)

    @pl.when(jnp.logical_and(jnp.logical_and(place > 0, place <= full), jnp.logical_not(swapped)))
    def _():
        hops(False)

    smalls[2].wait()
    factor = weights[0] / (modes * energies)

    def density(wave):
        return jnp.sum(wave * wave, axis=0, keepdims=True) * factor

    def own(part, carry):
        @pl.when(swapped)
        def _():
            for chunk in range(half):
                forward(part * half + chunk).wait_recv()

        wave = waves[jnp.where(swapped, 1, 0), pl.ds(part * half, half)].reshape(half * 2 * ROWS, orbitals)
        for block in reversed(range(blocks)):
            wave = combine(narrow_product(wave, high[block], low[block]), orbitals)
            charge[part, block : block + 1, :] = density(wave)
        return carry

    def own_at_end(part, carry):
        @pl.when(place == 0)
        def _():
            for chunk in range(half):
                pass_on(part * half + chunk).wait_recv()

        wave = waves[0, pl.ds(part * half, half)].reshape(half * 2 * ROWS, orbitals)
        for block in range(blocks):
            slot = 6 - block
            moved = combine(narrow_product(wave, high[slot], low[slot]), orbitals)
            charge[part, block : block + 1, :] = density(moved)
        return carry

    @pl.when(place > 1)
    def _():
        lax.fori_loop(0, 2, own, 0)

    @pl.when(place <= 1)
    def _():
        lax.fori_loop(0, 2, own_at_end, 0)

    width = orbitals // energies
    summed = charge[0] + charge[1]
    for target in range(energies):
        part_out[target, :blocks, :width] = summed[:, target * width : (target + 1) * width]

    def give(hop):
        other = lax.rem(energy + hop, energies)
        return pltpu.make_async_remote_copy(
            src_ref=part_out.at[other],
            dst_ref=part_in.at[hop],
            send_sem=part_send_sem.at[hop],
            recv_sem=part_recv_sem.at[hop],
            device_id=(other, place),
            device_id_type=MESH,
        )

    order = sorted(range(1, energies), key=lambda hop: -min(hop, energies - hop))
    for hop in order:
        give(hop).start()
    total = part_out[energy]
    for hop in reversed(order):
        give(hop).wait_recv()
        total = total + part_in[hop]
    out_ref[...] = total[:blocks, : orbitals // energies]
    for hop in range(1, energies):
        give(hop).wait_send()

    @pl.when(place > 0)
    def _():
        for chunk in range(chunks):
            pass_on(chunk).wait_send()

    @pl.when(swapped)
    def _():
        for chunk in range(chunks):
            forward(chunk).wait_send()
        for part in range(2):
            swap(part).wait_send()


def shards(places, energies, green_left, coupling, pattern, injection, weights):
    blocks, orbitals, _ = coupling.shape
    tiles = pattern.shape[1]
    modes = injection.shape[3]
    chunks = modes // ROWS
    sizes = (energies, places, blocks, orbitals, tiles, modes)
    return pl.pallas_call(
        functools.partial(kernel, sizes),
        out_shape=pltpu.VMEM((blocks, orbitals // energies), jnp.float32),
        in_specs=[pl.BlockSpec(memory_space=pltpu.HBM)] * 5,
        out_specs=pl.BlockSpec(memory_space=pltpu.VMEM),
        scratch_shapes=[
            pltpu.VMEM((blocks, 2, orbitals, orbitals), jnp.float32),
            pltpu.VMEM((blocks, orbitals, orbitals), jnp.float32),
            pltpu.VMEM(pattern.shape, jnp.int32),
            pltpu.VMEM((2, modes, orbitals), jnp.float32),
            pltpu.SMEM((1,), jnp.float32),
            pltpu.VMEM((7, orbitals, 2 * orbitals), jnp.bfloat16),
            pltpu.VMEM((7, orbitals, 2 * orbitals), jnp.bfloat16),
            pltpu.VMEM((2, chunks, 2 * ROWS, orbitals), jnp.float32),
            pltpu.VMEM((chunks, 2 * ROWS, orbitals), jnp.float32),
            pltpu.VMEM((2, orbitals, orbitals), jnp.float32),
            pltpu.VMEM((energies, 8, 128), jnp.float32),
            pltpu.VMEM((energies, 8, 128), jnp.float32),
            pltpu.VMEM((2, blocks, orbitals), jnp.float32),
            pltpu.SemaphoreType.DMA((2, blocks)),
            pltpu.SemaphoreType.DMA((3,)),
            pltpu.SemaphoreType.DMA((chunks,)),
            pltpu.SemaphoreType.DMA((chunks,)),
            pltpu.SemaphoreType.DMA((energies,)),
            pltpu.SemaphoreType.DMA((energies,)),
            pltpu.SemaphoreType.DMA((chunks,)),
            pltpu.SemaphoreType.DMA((chunks,)),
            pltpu.SemaphoreType.DMA((2,)),
            pltpu.SemaphoreType.DMA((2,)),
        ],
        compiler_params=pltpu.CompilerParams(
            collective_id=0, has_side_effects=True, vmem_limit_bytes=56 * 1024 * 1024
        ),
    )(green_left, coupling, pattern, jnp.swapaxes(injection, 2, 3), weights)


def solution(mesh):
    placed = (
        P("energy", "length", None, None, None),
        P("length", None, None),
        P("length", None, None),
        P("energy", None, None, None),
        P("energy"),
    )
    return jax.shard_map(
        functools.partial(shards, mesh.shape["length"], mesh.shape["energy"]),
        mesh=mesh,
        in_specs=placed,
        out_specs=P("length", "energy"),
        check_vma=False,
    )
```
